32 devices in a mesh: dp: 8 (over y, x, core), expert: 4 (over z), tensor: 1.
Axes of the slice: x: 2, y: 2, z: 4, core: 2. Of those that a mesh axis runs over, the one named last changes fastest.
Arguments:
- tokens: bfloat16 [2048, 4096], P(('dp', 'expert'), 'tensor'), may hold values from -6 to 6
- expert_ids: int32 [2048, 8], P(('dp', 'expert')), may hold values from 0 to 31, all different within a row; in each aligned block of 64 rows (0 to 63, 64 to 127, ...) at most 24 rows name the same one
- combine_weights: float32 [2048, 8], P(('dp', 'expert')), may hold values from 0.05 to 1
- topology: int32 [32, 12, 12], P(('dp', 'expert'), 'tensor'), may hold values from 0 to 31, all different within a row
- gate_blocks: bfloat16 [32, 12, 12, 128, 128], P(('dp', 'expert'), 'tensor'), may hold values from -0.15625 to 0.15625
- up_blocks: bfloat16 [32, 12, 12, 128, 128], P(('dp', 'expert'), 'tensor'), may hold values from -0.15625 to 0.15625
- down_blocks: bfloat16 [32, 12, 12, 128, 128], P(('dp', 'expert'), 'tensor'), may hold values from -0.25 to 0.25
Outputs:
- layer_out: bfloat16 [2048, 4096], P(('dp', 'expert'), 'tensor')
The draws below stay inside these ranges and needn't reach their ends.
Inputs may be any that keep to these rules, and one draw needn't show every extreme that they name: `expert_ids`: in each aligned block of 64 tokens (the tokens of one index of dp+expert), no expert is named more than 24 times, a bound that some block reaches; a token names 8 different experts. `topology`: each row names 12 different blocks; every block is named by some row.
All inputs are finite; a program needn't handle non-finite values.
Results may differ from the reference program's by a relative error of at most 0.0058.
Values may be sent and summed in bfloat16 or wider, within the bound.
No kernel may reach another device: no remote copies, remote signals or barrier semaphores. Data moves between devices by JAX's collectives and lax.ppermute only.
A program may use at most 256 MiB of HBM per device.

```python
import math
import jax
import jax.numpy as jnp
import numpy as np
from jax import lax

D = 4096
FF = 1536
TOP = 8
BLK = 128
KB = 12
TOK_DEV = 64
EXPERTS = 32
CAP = 24
TOKENS = 2048
N_TENSOR = 1


def levels(own_key, shape, shards, least, high):
    level, own = 1.0, jax.random.fold_in(own_key, 6)
    for axis_at, parts in shards:
        draws = jnp.exp(jax.random.uniform(jax.random.fold_in(own, axis_at), (parts,), jnp.float32, least / len(shards), high / len(shards)))
        level = level * jnp.repeat(draws, shape[axis_at] // parts).reshape([-1 if axis == axis_at else 1 for axis in range(len(shape))])
    return level


def different_ones(stream_key, rows, amount, top, lift):
    order = jax.random.permutation(jax.random.fold_in(stream_key, 1), amount)
    favour = order
    for power in range(3):
        favour = favour * favour // amount
    favour = favour * lift // amount
    tickets = jax.random.randint(jax.random.fold_in(stream_key, 2), (rows, amount), 0, 4096) + favour
    holders = jax.random.permutation(jax.random.fold_in(stream_key, 3), rows)[jnp.arange(amount) % rows]
    tickets = jnp.where(jnp.arange(rows)[:, None] == holders[None, :], 1 << 14, tickets)
    merit = tickets * amount + jnp.arange(amount)
    return lax.top_k(merit.astype(jnp.int32), top)[1].astype(jnp.int32)


def shared_out(own_key, own, number, rows, number_of, top, reach, slope):
    sequence = jax.random.permutation(own_key, number_of)
    heavy_load, common = portions_of(number_of, rows * top, reach, slope, True), portions_of(number_of, rows * top, reach, slope, False)
    places = jnp.arange(number_of)

    def named(tallies, rotation):
        used = int((tallies > 0).sum())
        fixed = max(1, used // 4)
        shifted = fixed + (places - fixed + rotation * (used - fixed)) % max(1, number_of - fixed)
        return jnp.zeros((number_of,), jnp.int32).at[sequence[jnp.where(places < fixed, places, shifted)]].set(jnp.asarray(tallies, jnp.int32))

    tallies = jnp.where(number % 4 == 0, named(heavy_load, number // 4), named(common, number - number // 4 - 1))
    mixed = jax.random.permutation(jax.random.fold_in(own, 3), number_of)
    source_of, receiver = mixed[0:number_of // 2 * 2:2], mixed[1:number_of // 2 * 2:2]
    room = jnp.minimum(tallies[source_of] - 1, reach - tallies[receiver]) // 2
    room = jnp.where((source_of == sequence[0]) | (receiver == sequence[0]) | (tallies[receiver] == 0), 0, jnp.maximum(room, 0))
    shifted = jax.random.randint(jax.random.fold_in(own, 4), (number_of // 2,), 0, 1 << 20) % (room + 1)
    tallies = tallies.at[source_of].add(-shifted).at[receiver].add(shifted)
    items = jnp.searchsorted(jnp.cumsum(tallies), jnp.arange(rows * top), side="right").astype(jnp.int32)
    listing = items.reshape(top, rows).T
    listing = listing[jax.random.permutation(jax.random.fold_in(own, 1), rows)]
    rotation = jax.random.randint(jax.random.fold_in(own, 2), (rows, 1), 0, top)
    return jnp.take_along_axis(listing, (jnp.arange(top)[None, :] + rotation) % top, axis=1)


def portions_of(number_of, total, limit, slope, full):
    loads = [(1 << 20) // math.isqrt(rank ** slope) + 1 for rank in range(1, number_of + 1)]
    largest = limit if full else min(limit, max(-(-total // number_of), total * loads[0] // sum(loads)))
    least = 1 if total - largest >= number_of - 1 else 0
    holding, spare = [largest] + [least] * (number_of - 1), total - largest - least * (number_of - 1)
    while spare > 0:
        candidates = [i for i in range(1, number_of) if holding[i] < largest] or [i for i in range(1, number_of) if holding[i] < limit]
        pool, remaining = sum([loads[i] for i in candidates]), spare
        for i in candidates:
            more = min(limit - holding[i], max(1, remaining * loads[i] // pool), spare)
            holding[i] = holding[i] + more
            spare = spare - more
    return np.array(holding)


def noise(key, extent, deviation, reach, shards=(), kind=jnp.bfloat16):
    gain = levels(key, extent, shards, -0.22, 0.18) if shards else 1.0
    values = jax.random.normal(key, extent, jnp.float32) * deviation * gain
    return jnp.minimum(jnp.maximum(values, -reach), reach).astype(kind)


def setup_inputs(seed: int = 0) -> dict:
    key_list = jax.random.split(jax.random.key(seed), 8)
    tokens = noise(key_list[0], (TOKENS, D), 1.0, 6.0, ((0, 32),))
    expert_ids_keys = jax.random.split(jax.random.fold_in(key_list[1], 1), TOKENS // TOK_DEV)
    expert_ids_turns = jax.random.permutation(jax.random.fold_in(key_list[1], 3), TOKENS // TOK_DEV)
    expert_ids = jax.vmap(lambda own, number: shared_out(jax.random.fold_in(key_list[1], 2), own, number, TOK_DEV, EXPERTS, TOP, CAP, 2))(expert_ids_keys, expert_ids_turns).reshape((TOKENS, TOP))
    combine_weights = jnp.clip(0.05 + 0.95 * jax.random.uniform(key_list[2], (TOKENS, TOP), jnp.float32) ** levels(key_list[2], (TOKENS, TOP), ((0, 32),), -0.2, 0.2), 0.05, 1.0)
    topology = different_ones(key_list[3], EXPERTS * (FF // BLK), D // BLK, KB, 0).reshape((EXPERTS, FF // BLK, KB))
    gate_blocks = noise(key_list[4], (EXPERTS, FF // BLK, KB, BLK, BLK), (KB * BLK) ** -0.5, 0.15625, ((0, 32),))
    up_blocks = noise(key_list[5], (EXPERTS, FF // BLK, KB, BLK, BLK), (KB * BLK) ** -0.5, 0.15625, ((0, 32),))
    down_blocks = noise(key_list[6], (EXPERTS, FF // BLK, KB, BLK, BLK), (FF * KB * BLK // D) ** -0.5, 0.25, ((0, 32),))
    return dict(tokens=tokens, expert_ids=expert_ids, combine_weights=combine_weights, topology=topology, gate_blocks=gate_blocks, up_blocks=up_blocks, down_blocks=down_blocks)


def slot_numbers(expert_ids):
    groups = expert_ids.shape[0] // TOK_DEV
    picked_ids = expert_ids.reshape(groups, TOK_DEV * TOP)
    onehot = (picked_ids[:, :, None] == jnp.arange(EXPERTS, dtype=jnp.int32)[None, None, :]).astype(jnp.int32)
    before = jnp.cumsum(onehot, axis=1) - onehot
    return jnp.sum(before * onehot, axis=2).reshape(expert_ids.shape).astype(jnp.int32)


def expert_rows(rows, layout_ids, gate_part, up_part, down_part):
    row_count = rows.shape[0]
    blocked = rows.reshape(row_count, D // BLK, BLK).astype(jnp.float32)
    local_blocks = FF // BLK // N_TENSOR
    placer = (layout_ids[:, :, None] == jnp.arange(D // BLK, dtype=jnp.int32)[None, None, :]).astype(jnp.float32)
    total_out = jnp.zeros((row_count, D // BLK, BLK), jnp.float32)
    for quarter in range(N_TENSOR):
        start_block = quarter * local_blocks
        end_block = start_block + local_blocks
        chosen = layout_ids[start_block:end_block].reshape(-1).astype(jnp.int32)
        picked = jnp.take(blocked, chosen, axis=1).reshape(row_count, local_blocks, KB, BLK)
        gate_proj = jnp.einsum('rhkc,hkcf->rhf', picked, gate_part[start_block:end_block].astype(jnp.float32))
        up_proj = jnp.einsum('rhkc,hkcf->rhf', picked, up_part[start_block:end_block].astype(jnp.float32))
        hidden = (jax.nn.silu(gate_proj) * up_proj).astype(jnp.bfloat16)
        pieces = jnp.einsum('rhf,hkfc->rhkc', hidden.astype(jnp.float32), down_part[start_block:end_block].astype(jnp.float32))
        partial_value = jnp.einsum('rhkc,hkb->rbc', pieces, placer[start_block:end_block], precision=lax.Precision.HIGHEST)
        rounded = lax.optimization_barrier(partial_value.astype(jnp.bfloat16))
        total_out = total_out + rounded.astype(jnp.float32)
    return total_out.reshape(row_count, D)


def reference(tokens, expert_ids, combine_weights, topology, gate_blocks, up_blocks, down_blocks):
    groups = TOKENS // TOK_DEV
    slot_index = slot_numbers(expert_ids)
    owner_group = (jnp.arange(TOKENS, dtype=jnp.int32) // TOK_DEV).astype(jnp.int32)
    positions = (owner_group[:, None] * CAP + slot_index).astype(jnp.int32)
    token_index = jnp.broadcast_to(jnp.arange(TOKENS, dtype=jnp.int32)[:, None], (TOKENS, TOP))
    slot_table = jnp.full((EXPERTS, groups * CAP), TOKENS, jnp.int32)
    slot_table = slot_table.at[expert_ids.reshape(-1), positions.reshape(-1)].set(token_index.reshape(-1))
    weight_table = jnp.zeros((EXPERTS, groups * CAP), jnp.float32)
    weight_table = weight_table.at[expert_ids.reshape(-1), positions.reshape(-1)].set(combine_weights.reshape(-1))
    padded = jnp.concatenate([tokens, jnp.zeros((1, D), jnp.bfloat16)], axis=0)

    def per_expert(running, scanned):
        row_index, weights, layout_ids, gate_part, up_part, down_part = scanned
        results = expert_rows(padded[row_index], layout_ids, gate_part, up_part, down_part)
        return running.at[row_index].add(weights[:, None] * results), None

    initial = jnp.zeros((TOKENS + 1, D), jnp.float32)
    summed_out, _ = lax.scan(per_expert, initial, (slot_table, weight_table, topology, gate_blocks, up_blocks, down_blocks))
    return summed_out[:TOKENS].astype(jnp.bfloat16)
```

```python
import functools

import jax
import jax.numpy as jnp
from jax import lax
from jax.experimental import pallas as pl
from jax.experimental.pallas import tpu as pltpu
from jax.sharding import PartitionSpec as P

TOP = 8
BLK = 128
BF16 = jnp.bfloat16
F32 = jnp.float32
VMEM_LIMIT = 48 * 1024 * 1024


def slot_numbers(expert_ids, experts):
    flat_ids = expert_ids.reshape(-1)
    onehot = (flat_ids[:, None] == jnp.arange(experts, dtype=jnp.int32)[None, :]).astype(jnp.int32)
    before = jnp.cumsum(onehot, axis=0) - onehot
    return jnp.sum(before * onehot, axis=1).reshape(expert_ids.shape)


def combine_rows(flat_rows, target, combine_weights):
    total = jnp.zeros((target.shape[0], flat_rows.shape[1]), jnp.float32)
    for pick in range(target.shape[1]):
        chosen = jnp.take(flat_rows, target[:, pick], axis=0)
        total = total + combine_weights[:, pick][:, None] * chosen
    return total


def general_device(tokens, expert_ids, combine_weights, topology, gate_blocks, up_blocks, down_blocks):
    experts = lax.axis_size(("dp", "expert"))
    width = tokens.shape[1] * lax.axis_size("tensor")
    tok_rows = tokens.shape[0]
    capacity = min(tok_rows, 3 * tok_rows * TOP // (2 * experts))
    slot_index = slot_numbers(expert_ids, experts)
    target = expert_ids * capacity + slot_index
    places = jnp.arange(experts * capacity, dtype=jnp.int32)
    matches = target[None, :, :] == places[:, None, None]
    dispatch = jnp.any(matches, axis=2).astype(BF16)
    outgoing = jnp.dot(dispatch, tokens, preferred_element_type=F32).astype(BF16)
    outgoing = outgoing.reshape(experts, capacity, tokens.shape[1])
    arrived = lax.all_to_all(outgoing, ("dp", "expert"), split_axis=0, concat_axis=0, tiled=True)
    expert_in = lax.all_gather(arrived, "tensor", axis=2, tiled=True)
    row_count = experts * capacity
    layout_ids = topology[0]
    blocked = expert_in.reshape(row_count, width // BLK, BLK)
    width_ids = jnp.arange(width // BLK, dtype=jnp.int32)
    partial_value = jnp.zeros((row_count, width // BLK, BLK), F32)
    for block in range(layout_ids.shape[0]):
        chosen = layout_ids[block]
        picked = jnp.take(blocked, chosen, axis=1)
        gate_proj = jnp.einsum("rkc,kcf->rf", picked, gate_blocks[0, block], preferred_element_type=F32)
        up_proj = jnp.einsum("rkc,kcf->rf", picked, up_blocks[0, block], preferred_element_type=F32)
        hidden = (jax.nn.silu(gate_proj) * up_proj).astype(BF16)
        pieces = jnp.einsum("rf,kfc->rkc", hidden, down_blocks[0, block], preferred_element_type=F32)
        placer = (chosen[:, None] == width_ids[None, :]).astype(F32)
        partial_value = partial_value + jnp.einsum(
            "rkc,kb->rbc", pieces, placer, precision=lax.Precision.HIGHEST
        )
    partial_low = lax.optimization_barrier(partial_value.reshape(experts, capacity, width).astype(BF16))
    shares = lax.all_to_all(
        partial_low.reshape(1, experts, capacity, width), "tensor", split_axis=3, concat_axis=0, tiled=True
    )
    summed = jnp.sum(shares.astype(F32), axis=0)
    returned_rows = lax.all_to_all(summed, ("dp", "expert"), split_axis=0, concat_axis=0, tiled=True)
    flat_rows = returned_rows.reshape(row_count, returned_rows.shape[2])
    return combine_rows(flat_rows, target, combine_weights).astype(BF16)


CORE, XBIT, YBIT = 1, 2, 4
PAIRS = [(0, 1), (1, 0), (2, 3), (3, 2)]
MIDDLES = [(1, 2), (2, 1)]
OUTWARD = [(1, 0), (2, 3)]
INWARD = [(0, 1), (3, 2)]


def flip(value, bit):
    return lax.ppermute(value, "dp", [(i, i ^ bit) for i in range(lax.axis_size("dp"))])


def along(value, pairs):
    return lax.ppermute(value, "expert", pairs)


def add(*values):
    return functools.reduce(lambda a, b: a + b, [v.astype(F32) for v in values]).astype(BF16)


def select_kernel(width, experts, cap, ids, a, b, c, d, own, send, hot):
    rows = a.shape[0]
    slots = 4 * cap
    lane = lax.broadcasted_iota(jnp.int32, (rows, BLK), 1)
    place = lax.broadcasted_iota(jnp.int32, (rows, 2 * slots), 1)
    parts = []
    for n, ref in enumerate((a, b, c, d)):
        meta = ref[:, width:].astype(F32)
        match = None
        for which in range(2):
            rank = jnp.sum(jnp.where(lane == 3 * experts + ids[which], meta, 0.0), axis=1, keepdims=True).astype(jnp.int32)
            goal = jnp.where(rank >= 0, rank + (which * slots + n * cap), -1)
            here = place == goal
            match = here if match is None else match | here
        parts.append(jnp.where(match, 1.0, 0.0))
    hot_t = jnp.concatenate(parts, axis=0).astype(BF16)
    hot[...] = hot_t
    step = 3 * BLK
    for at in range(0, own.shape[1], step):
        cols = slice(at, at + step)
        block = jnp.concatenate([a[:, cols], b[:, cols], c[:, cols], d[:, cols]], axis=0)
        picked = lax.dot_general(hot_t, block, (((0,), (0,)), ((), ())), preferred_element_type=F32).astype(BF16)
        own[:, cols] = picked[:slots]
        send[:, cols] = picked[slots:]


def select(ids, blocks, width, experts, cap):
    rows, full = blocks[0].shape
    return pl.pallas_call(
        functools.partial(select_kernel, width, experts, cap),
        out_shape=(
            jax.ShapeDtypeStruct((4 * cap, full), BF16),
            jax.ShapeDtypeStruct((4 * cap, full), BF16),
            jax.ShapeDtypeStruct((4 * rows, 8 * cap), BF16),
        ),
        in_specs=[pl.BlockSpec(memory_space=pltpu.SMEM)] + [pl.BlockSpec(memory_space=pltpu.VMEM)] * 4,
        out_specs=(pl.BlockSpec(memory_space=pltpu.VMEM),) * 3,
        compiler_params=pltpu.CompilerParams(vmem_limit_bytes=VMEM_LIMIT),
        name="select_rows",
    )(ids, *blocks)


def expert_kernel(count, width, experts, ids, topo, *refs):
    inputs, (gate, up, down) = refs[:count], refs[count : count + 3]
    outputs, (x, total) = refs[count + 3 : 2 * count + 3], refs[2 * count + 3 :]
    h = pl.program_id(0)
    rows = inputs[0].shape[0]

    @pl.when(h == 0)
    def _():
        for n, ref in enumerate(inputs):
            x[n * rows : (n + 1) * rows, :] = ref[:, :width]
        total[...] = jnp.zeros_like(total)

    kb = gate.shape[2]
    cols = [pl.ds(pl.multiple_of(topo[h, i] * BLK, BLK), BLK) for i in range(kb)]
    picked = jnp.concatenate([x[:, c] for c in cols], axis=1)
    weights = jnp.concatenate(
        [gate[0, 0].reshape(kb * BLK, BLK), up[0, 0].reshape(kb * BLK, BLK)], axis=1
    )
    both = jnp.dot(picked, weights, preferred_element_type=F32)
    gate_proj, up_proj = both[:, :BLK], both[:, BLK:]
    hidden = (gate_proj / (1.0 + jnp.exp(-gate_proj)) * up_proj).astype(BF16)
    for i in range(0, kb, 2):
        pair = jnp.concatenate([down[0, 0, i], down[0, 0, i + 1]], axis=1)
        pieces = jnp.dot(hidden, pair, preferred_element_type=F32)
        total[:, cols[i]] += pieces[:, :BLK]
        total[:, cols[i + 1]] += pieces[:, BLK:]

    @pl.when(h == pl.num_programs(0) - 1)
    def _():
        lane = lax.broadcasted_iota(jnp.int32, (rows, BLK), 1)
        mine = (lax.rem(lane, experts) == ids[0]) & (lane < 3 * experts)
        for n, (ref, out) in enumerate(zip(inputs, outputs)):
            meta = ref[:, width:].astype(F32)
            weight = jnp.sum(jnp.where(mine, meta, 0.0), axis=1, keepdims=True)
            out[...] = (total[n * rows : (n + 1) * rows, :] * weight).astype(BF16)


def expert(ids, topo, inputs, gate, up, down, width, experts):
    count, rows = len(inputs), inputs[0].shape[0]
    _, blocks, kb, _, _ = gate.shape
    spec = pl.BlockSpec((1, 1, kb, BLK, BLK), lambda h: (0, h, 0, 0, 0))
    return pl.pallas_call(
        functools.partial(expert_kernel, count, width, experts),
        grid=(blocks,),
        out_shape=[jax.ShapeDtypeStruct((rows, width), BF16)] * count,
        in_specs=[pl.BlockSpec(memory_space=pltpu.SMEM)] * 2
        + [pl.BlockSpec(v.shape, lambda h: (0, 0)) for v in inputs]
        + [spec] * 3,
        out_specs=[pl.BlockSpec((rows, width), lambda h: (0, 0))] * count,
        scratch_shapes=[pltpu.VMEM((count * rows, width), BF16), pltpu.VMEM((count * rows, width), F32)],
        compiler_params=pltpu.CompilerParams(vmem_limit_bytes=VMEM_LIMIT),
        name="expert_rows",
    )(ids, topo, *inputs, gate, up, down)


def spread_kernel(hot, own, back, a, b, c, d):
    rows = a.shape[0]
    step = 4 * BLK
    for at in range(0, own.shape[1], step):
        cols = slice(at, at + step)
        both = jnp.concatenate([own[:, cols], back[:, cols]], axis=0)
        sums = jnp.dot(hot[...], both, preferred_element_type=F32).astype(BF16)
        for n, ref in enumerate((a, b, c, d)):
            ref[:, cols] = sums[n * rows : (n + 1) * rows]


def spread(hot, own, back):
    rows, width = hot.shape[0] // 4, own.shape[1]
    return pl.pallas_call(
        spread_kernel,
        out_shape=[jax.ShapeDtypeStruct((rows, width), BF16)] * 4,
        in_specs=[pl.BlockSpec(memory_space=pltpu.VMEM)] * 3,
        out_specs=[pl.BlockSpec(memory_space=pltpu.VMEM)] * 4,
        compiler_params=pltpu.CompilerParams(vmem_limit_bytes=VMEM_LIMIT),
        name="spread_rows",
    )(hot, own, back)


def with_meta(tokens, expert_ids, combine_weights, experts):
    rows = tokens.shape[0]
    named = expert_ids[:, :, None] == jnp.arange(experts, dtype=jnp.int32)[None, None, :]
    weight = jnp.sum(jnp.where(named, combine_weights[:, :, None], 0.0), axis=1)
    chosen = jnp.any(named, axis=1)
    earlier = jnp.tril(jnp.ones((rows, rows), BF16), -1)
    rank = jnp.dot(earlier, chosen.astype(BF16), preferred_element_type=F32)
    rank = jnp.where(chosen, rank, -1.0)
    high = lax.reduce_precision(weight, 8, 7)
    middle = lax.reduce_precision(weight - high, 8, 7)
    low = weight - high - middle
    return jnp.concatenate([tokens] + [v.astype(BF16) for v in (high, middle, low, rank)], axis=1)


GROUPS = ((0, 1), (2, 3))


def line_device(tokens, expert_ids, combine_weights, topology, gate_blocks, up_blocks, down_blocks):
    experts = lax.axis_size(("dp", "expert"))
    rows, width = tokens.shape
    cap = min(rows, 3 * rows * TOP // (2 * experts))
    dp, z = lax.axis_index("dp"), lax.axis_index("expert")
    line = lax.axis_size("expert")
    ids = jnp.stack([dp * line + z, (dp ^ CORE) * line + z]).astype(jnp.int32)
    middle = (z == 1) | (z == 2)
    topo = topology[0]

    own = with_meta(tokens, expert_ids, combine_weights, experts)
    from_pair = along(own, PAIRS)
    from_middle = along(own, MIDDLES)
    second = jnp.where(middle, along(from_pair, MIDDLES), along(from_middle, OUTWARD))
    third = jnp.where(middle, from_middle, along(second, OUTWARD))
    layers = [own, from_pair, second, third]

    returned = {}
    for group in GROUPS:
        hots, mine, theirs = [], [], []
        for k in group:
            here = layers[k]
            by_x, by_y = flip(here, XBIT), flip(here, YBIT)
            across = flip(by_y, XBIT) if k % 2 == 0 else flip(by_x, YBIT)
            kept, sent, hot = select(ids, [here, by_x, by_y, across], width, experts, cap)
            hots.append(hot)
            mine.append(kept)
            theirs.append(flip(sent, CORE))
        results = expert(ids, topo, mine + theirs, gate_blocks, up_blocks, down_blocks, width, experts)
        count = len(group)
        for n, k in reversed(list(enumerate(group))):
            back = flip(results[count + n], CORE)
            here, to_x, to_y, across = spread(hots[n], results[n], back)
            if k % 2 == 0:
                to_y = add(to_y, flip(across, XBIT))
            else:
                to_x = add(to_x, flip(across, YBIT))
            returned[k] = (here, flip(to_x, XBIT), flip(to_y, YBIT))

    third = add(*returned[3])
    second = add(*returned[2])
    end_third, end_second = along(third, INWARD), along(second, INWARD)
    second = add(second, end_third)
    third = add(third, end_second)
    first = add(*returned[1], along(second, MIDDLES))
    last = along(third, MIDDLES)
    return add(*returned[0], last, along(first, PAIRS))


def solution(mesh):
    line = mesh.shape["dp"] == 8 and mesh.shape["expert"] == 4 and mesh.shape["tensor"] == 1
    return jax.shard_map(
        line_device if line else general_device,
        mesh=mesh,
        in_specs=(
            P(("dp", "expert"), "tensor"),
            P(("dp", "expert"), None),
            P(("dp", "expert"), None),
            P(("dp", "expert"), "tensor", None),
            P(("dp", "expert"), "tensor", None, None, None),
            P(("dp", "expert"), "tensor", None, None, None),
            P(("dp", "expert"), "tensor", None, None, None),
        ),
        out_specs=P(("dp", "expert"), "tensor"),
        check_vma=False,
    )
```

```python
import functools

import jax
import jax.numpy as jnp
from jax import lax
from jax.experimental import pallas as pl
from jax.experimental.pallas import tpu as pltpu
from jax.sharding import PartitionSpec as P

TOP = 8
BLK = 128
BF16 = jnp.bfloat16
F32 = jnp.float32
VMEM_LIMIT = 48 * 1024 * 1024


def slot_numbers(expert_ids, experts):
    flat_ids = expert_ids.reshape(-1)
    onehot = (flat_ids[:, None] == jnp.arange(experts, dtype=jnp.int32)[None, :]).astype(jnp.int32)
    before = jnp.cumsum(onehot, axis=0) - onehot
    return jnp.sum(before * onehot, axis=1).reshape(expert_ids.shape)


def combine_rows(flat_rows, target, combine_weights):
    total = jnp.zeros((target.shape[0], flat_rows.shape[1]), jnp.float32)
    for pick in range(target.shape[1]):
        chosen = jnp.take(flat_rows, target[:, pick], axis=0)
        total = total + combine_weights[:, pick][:, None] * chosen
    return total


def general_device(tokens, expert_ids, combine_weights, topology, gate_blocks, up_blocks, down_blocks):
    experts = lax.axis_size(("dp", "expert"))
    width = tokens.shape[1] * lax.axis_size("tensor")
    tok_rows = tokens.shape[0]
    capacity = min(tok_rows, 3 * tok_rows * TOP // (2 * experts))
    slot_index = slot_numbers(expert_ids, experts)
    target = expert_ids * capacity + slot_index
    places = jnp.arange(experts * capacity, dtype=jnp.int32)
    matches = target[None, :, :] == places[:, None, None]
    dispatch = jnp.any(matches, axis=2).astype(BF16)
    outgoing = jnp.dot(dispatch, tokens, preferred_element_type=F32).astype(BF16)
    outgoing = outgoing.reshape(experts, capacity, tokens.shape[1])
    arrived = lax.all_to_all(outgoing, ("dp", "expert"), split_axis=0, concat_axis=0, tiled=True)
    expert_in = lax.all_gather(arrived, "tensor", axis=2, tiled=True)
    row_count = experts * capacity
    layout_ids = topology[0]
    blocked = expert_in.reshape(row_count, width // BLK, BLK)
    width_ids = jnp.arange(width // BLK, dtype=jnp.int32)
    partial_value = jnp.zeros((row_count, width // BLK, BLK), F32)
    for block in range(layout_ids.shape[0]):
        chosen = layout_ids[block]
        picked = jnp.take(blocked, chosen, axis=1)
        gate_proj = jnp.einsum("rkc,kcf->rf", picked, gate_blocks[0, block], preferred_element_type=F32)
        up_proj = jnp.einsum("rkc,kcf->rf", picked, up_blocks[0, block], preferred_element_type=F32)
        hidden = (jax.nn.silu(gate_proj) * up_proj).astype(BF16)
        pieces = jnp.einsum("rf,kfc->rkc", hidden, down_blocks[0, block], preferred_element_type=F32)
        placer = (chosen[:, None] == width_ids[None, :]).astype(F32)
        partial_value = partial_value + jnp.einsum(
            "rkc,kb->rbc", pieces, placer, precision=lax.Precision.HIGHEST
        )
    partial_low = lax.optimization_barrier(partial_value.reshape(experts, capacity, width).astype(BF16))
    shares = lax.all_to_all(
        partial_low.reshape(1, experts, capacity, width), "tensor", split_axis=3, concat_axis=0, tiled=True
    )
    summed = jnp.sum(shares.astype(F32), axis=0)
    returned_rows = lax.all_to_all(summed, ("dp", "expert"), split_axis=0, concat_axis=0, tiled=True)
    flat_rows = returned_rows.reshape(row_count, returned_rows.shape[2])
    return combine_rows(flat_rows, target, combine_weights).astype(BF16)


CORE, XBIT, YBIT = 1, 2, 4
FLIPS = (0, XBIT, YBIT, XBIT | YBIT)
XOR = {k: [(i, i ^ k) for i in range(4)] for k in (1, 2, 3)}
HALVES = 2


def flip(value, bit):
    return lax.ppermute(value, "dp", [(i, i ^ bit) for i in range(lax.axis_size("dp"))])


def along(value, pairs):
    return lax.ppermute(value, "expert", pairs)


def exchange(messages):
    across = flip(messages[3], FLIPS[3])
    return [messages[0], flip(messages[1], FLIPS[1]), flip(messages[2], FLIPS[2]), across]


def hold(values, after):
    return list(lax.optimization_barrier(tuple(values) + tuple(after))[: len(values)])


def both(arrived, others):
    held = hold([arrived[3], arrived[1], arrived[2], arrived[0]] + list(others), [])
    return [held[3], held[1], held[2], held[0]], held[4:]


def add(*values):
    return functools.reduce(lambda a, b: a + b, [v.astype(F32) for v in values]).astype(BF16)


def column(meta, lane):
    at = lax.broadcasted_iota(jnp.int32, meta.shape, 1)
    return jnp.sum(jnp.where(at == lane, meta, 0.0), axis=1, keepdims=True)


def slots_of(meta, half, ids, experts, cap, weighted):
    place = lax.broadcasted_iota(jnp.int32, (meta.shape[0], len(FLIPS) * HALVES * cap), 1)
    terms = [0.0] * (3 if weighted else 1)
    for n in range(len(FLIPS)):
        rank = column(meta, 3 * experts + ids[n]).astype(jnp.int32)
        here = place == jnp.where(rank >= 0, rank + (n * HALVES + half) * cap, -1)
        for t in range(len(terms)):
            terms[t] = jnp.where(here, column(meta, t * experts + ids[n]) if weighted else 1.0, terms[t])
    return terms


def select_kernel(width, experts, cap, ids, near, far, *outs):
    hot = jnp.concatenate(
        [slots_of(ref[:, width:].astype(F32), half, ids, experts, cap, False)[0] for half, ref in enumerate((near, far))],
        axis=0,
    ).astype(BF16)
    each = HALVES * cap
    step = 4 * BLK
    for at in range(0, width, step):
        cols = slice(at, at + step)
        block = jnp.concatenate([near[:, cols], far[:, cols]], axis=0)
        picked = lax.dot_general(hot, block, (((0,), (0,)), ((), ())), preferred_element_type=F32).astype(BF16)
        for n, out in enumerate(outs):
            out[:, cols] = picked[n * each : (n + 1) * each]


def select(ids, near, far, width, experts, cap):
    return pl.pallas_call(
        functools.partial(select_kernel, width, experts, cap),
        out_shape=[jax.ShapeDtypeStruct((HALVES * cap, width), BF16)] * len(FLIPS),
        in_specs=[pl.BlockSpec(memory_space=pltpu.SMEM)] + [pl.BlockSpec(memory_space=pltpu.VMEM)] * 2,
        out_specs=[pl.BlockSpec(memory_space=pltpu.VMEM)] * len(FLIPS),
        compiler_params=pltpu.CompilerParams(vmem_limit_bytes=VMEM_LIMIT),
        name="select_rows",
    )(ids, near, far)


def combine_kernel(width, experts, cap, ids, near, far, *refs):
    rows, (mine, theirs) = refs[:4], refs[4:]
    halves = [slots_of(ref[:, width:].astype(F32), half, ids, experts, cap, True) for half, ref in enumerate((near, far))]
    terms = [jnp.concatenate(pair, axis=0).astype(BF16) for pair in zip(*halves)]
    tokens = near.shape[0]
    step = 4 * BLK
    for at in range(0, width, step):
        cols = slice(at, at + step)
        block = jnp.concatenate([ref[:, cols] for ref in rows], axis=0)
        total = functools.reduce(
            lambda a, b: a + b, [jnp.dot(term, block, preferred_element_type=F32) for term in terms]
        )
        mine[:, cols] = total[:tokens]
        theirs[:, cols] = total[tokens:].astype(BF16)


def combine(ids, near, far, rows, width, experts, cap):
    tokens = near.shape[0]
    return pl.pallas_call(
        functools.partial(combine_kernel, width, experts, cap),
        out_shape=[jax.ShapeDtypeStruct((tokens, width), F32), jax.ShapeDtypeStruct((tokens, width), BF16)],
        in_specs=[pl.BlockSpec(memory_space=pltpu.SMEM)] + [pl.BlockSpec(memory_space=pltpu.VMEM)] * 6,
        out_specs=[pl.BlockSpec(memory_space=pltpu.VMEM)] * 2,
        compiler_params=pltpu.CompilerParams(vmem_limit_bytes=VMEM_LIMIT),
        name="combine_rows",
    )(ids, near, far, *rows)


def expert_kernel(count, topo, *refs):
    inputs, (gate, up, down) = refs[:count], refs[count : count + 3]
    outputs, (x, total) = refs[count + 3 : 2 * count + 3], refs[2 * count + 3 :]
    h = pl.program_id(0)
    rows = inputs[0].shape[0]

    @pl.when(h == 0)
    def _():
        for n, ref in enumerate(inputs):
            x[n * rows : (n + 1) * rows, :] = ref[...]
        total[...] = jnp.zeros_like(total)

    _, each, kb, _, _ = gate.shape
    cols = [[pl.ds(pl.multiple_of(topo[h * each + n, i] * BLK, BLK), BLK) for i in range(kb)] for n in range(each)]
    hidden = []
    for n in range(each):
        picked = jnp.concatenate([x[:, c] for c in cols[n]], axis=1)
        weights = jnp.concatenate([gate[0, n].reshape(kb * BLK, BLK), up[0, n].reshape(kb * BLK, BLK)], axis=1)
        both = jnp.dot(picked, weights, preferred_element_type=F32)
        gate_proj, up_proj = both[:, :BLK], both[:, BLK:]
        hidden.append((gate_proj / (1.0 + jnp.exp(-gate_proj)) * up_proj).astype(BF16))
    for n in range(each):
        for i in range(0, kb, 2):
            pair = jnp.concatenate([down[0, n, i], down[0, n, i + 1]], axis=1)
            pieces = jnp.dot(hidden[n], pair, preferred_element_type=F32)
            total[:, cols[n][i]] += pieces[:, :BLK]
            total[:, cols[n][i + 1]] += pieces[:, BLK:]

    @pl.when(h == pl.num_programs(0) - 1)
    def _():
        for n, out in enumerate(outputs):
            out[...] = total[n * rows : (n + 1) * rows, :].astype(BF16)


def expert(topo, inputs, weights):
    count, (rows, width) = len(inputs), inputs[0].shape
    _, blocks, kb, _, _ = weights[0].shape
    each = 3
    spec = pl.BlockSpec((1, each, kb, BLK, BLK), lambda h: (0, h, 0, 0, 0))
    whole = pl.BlockSpec((rows, width), lambda h: (0, 0))
    return pl.pallas_call(
        functools.partial(expert_kernel, count),
        grid=(blocks // each,),
        out_shape=[jax.ShapeDtypeStruct((rows, width), BF16)] * count,
        in_specs=[pl.BlockSpec(memory_space=pltpu.SMEM)] + [whole] * count + [spec] * 3,
        out_specs=[whole] * count,
        scratch_shapes=[pltpu.VMEM((count * rows, width), BF16), pltpu.VMEM((count * rows, width), F32)],
        compiler_params=pltpu.CompilerParams(vmem_limit_bytes=VMEM_LIMIT),
        name="expert_rows",
    )(topo, *inputs, *weights)


def with_meta(tokens, expert_ids, combine_weights, experts):
    rows = tokens.shape[0]
    named = expert_ids[:, :, None] == jnp.arange(experts, dtype=jnp.int32)[None, None, :]
    weight = jnp.sum(jnp.where(named, combine_weights[:, :, None], 0.0), axis=1)
    chosen = jnp.any(named, axis=1)
    earlier = jnp.tril(jnp.ones((rows, rows), BF16), -1)
    rank = jnp.dot(earlier, chosen.astype(BF16), preferred_element_type=F32)
    rank = jnp.where(chosen, rank, -1.0)
    high = lax.reduce_precision(weight, 8, 7)
    middle = lax.reduce_precision(weight - high, 8, 7)
    low = weight - high - middle
    return jnp.concatenate([tokens] + [v.astype(BF16) for v in (high, middle, low, rank)], axis=1)


def line_device(tokens, expert_ids, combine_weights, topology, gate_blocks, up_blocks, down_blocks):
    experts = lax.axis_size(("dp", "expert"))
    rows, width = tokens.shape
    cap = min(rows, 3 * rows * TOP // (2 * experts))
    dp, z = lax.axis_index("dp"), lax.axis_index("expert")
    ids = jnp.stack([(dp ^ bit) * lax.axis_size("expert") + z for bit in FLIPS]).astype(jnp.int32)
    topo = topology[0]
    weights = (gate_blocks, up_blocks, down_blocks)

    def chosen(near):
        far = flip(near, CORE)
        return (near, far), list(select(ids, near, far, width, experts, cap))

    def joined(pair, rows):
        mine, theirs = combine(ids, *pair, rows, width, experts, cap)
        return mine, flip(theirs, CORE)

    own = with_meta(tokens, expert_ids, combine_weights, experts)
    first, second = along(own, XOR[1]), along(own, XOR[2])
    pair0, out0 = chosen(own)

    in0 = exchange(out0)
    in0, (first, second, late) = both(in0, [first, second, own])
    pair1, out1 = chosen(first)

    in1 = exchange(out1)
    third = along(late, XOR[3])
    pair2, out2 = chosen(second)
    in0, out2 = both(in0, out2)
    back0 = expert(topo, in0, weights)
    in1, (third, *rest) = both(in1, [third] + list(out2) + list(back0))
    out2, back0 = rest[:4], rest[4:]

    in2 = exchange(out2)
    pair3, out3 = chosen(third)
    in1, out3 = both(in1, out3)
    back1 = expert(topo, in1, weights)
    in2, rest = both(in2, list(out3) + list(back1))
    out3, back1 = rest[:4], rest[4:]

    in3 = exchange(out3)
    back2 = expert(topo, in2, weights)
    in3, back2 = both(in3, back2)

    got2 = exchange(back2)
    back3 = expert(topo, in3, weights)
    got2, back3 = both(got2, back3)

    got3 = exchange(back3)
    mine2, theirs2 = joined(pair2, got2)
    sum2 = add(mine2, theirs2)
    got3, back1 = both(got3, back1)

    got1 = exchange(back1)
    far2 = along(sum2, XOR[2])
    mine3, theirs3 = joined(pair3, got3)
    mine3, theirs3, far2 = hold([mine3, theirs3, far2], [])
    sum3 = add(mine3, theirs3)
    got1, back0 = both(got1, back0)

    got0 = exchange(back0)
    far3 = along(sum3, XOR[3])
    mine1, theirs1 = joined(pair1, got1)
    mine1, theirs1, far3 = hold([mine1, theirs1, far3], [])
    sum1 = add(mine1, theirs1)
    far1 = along(sum1, XOR[1])
    mine0, theirs0 = joined(pair0, got0)
    return add(mine0, theirs0, far1, far2, far3)


def solution(mesh):
    line = mesh.shape["dp"] == 8 and mesh.shape["expert"] == 4 and mesh.shape["tensor"] == 1
    return jax.shard_map(
        line_device if line else general_device,
        mesh=mesh,
        in_specs=(
            P(("dp", "expert"), "tensor"),
            P(("dp", "expert"), None),
            P(("dp", "expert"), None),
            P(("dp", "expert"), "tensor", None),
            P(("dp", "expert"), "tensor", None, None, None),
            P(("dp", "expert"), "tensor", None, None, None),
            P(("dp", "expert"), "tensor", None, None, None),
        ),
        out_specs=P(("dp", "expert"), "tensor"),
        check_vma=False,
    )
```

```python
import functools

import jax
import jax.numpy as jnp
from jax import lax
from jax.experimental import pallas as pl
from jax.experimental.pallas import tpu as pltpu
from jax.sharding import PartitionSpec as P

TOP = 8
BLK = 128
BF16 = jnp.bfloat16
F32 = jnp.float32
VMEM_LIMIT = 16 * 1024 * 1024
EXPERT_VMEM_LIMIT = 28 * 1024 * 1024


def slot_numbers(expert_ids, experts):
    flat_ids = expert_ids.reshape(-1)
    onehot = (flat_ids[:, None] == jnp.arange(experts, dtype=jnp.int32)[None, :]).astype(jnp.int32)
    before = jnp.cumsum(onehot, axis=0) - onehot
    return jnp.sum(before * onehot, axis=1).reshape(expert_ids.shape)


def combine_rows(flat_rows, target, combine_weights):
    total = jnp.zeros((target.shape[0], flat_rows.shape[1]), jnp.float32)
    for pick in range(target.shape[1]):
        chosen = jnp.take(flat_rows, target[:, pick], axis=0)
        total = total + combine_weights[:, pick][:, None] * chosen
    return total


def general_device(tokens, expert_ids, combine_weights, topology, gate_blocks, up_blocks, down_blocks):
    experts = lax.axis_size(("dp", "expert"))
    width = tokens.shape[1] * lax.axis_size("tensor")
    tok_rows = tokens.shape[0]
    capacity = min(tok_rows, 3 * tok_rows * TOP // (2 * experts))
    slot_index = slot_numbers(expert_ids, experts)
    target = expert_ids * capacity + slot_index
    places = jnp.arange(experts * capacity, dtype=jnp.int32)
    matches = target[None, :, :] == places[:, None, None]
    dispatch = jnp.any(matches, axis=2).astype(BF16)
    outgoing = jnp.dot(dispatch, tokens, preferred_element_type=F32).astype(BF16)
    outgoing = outgoing.reshape(experts, capacity, tokens.shape[1])
    arrived = lax.all_to_all(outgoing, ("dp", "expert"), split_axis=0, concat_axis=0, tiled=True)
    expert_in = lax.all_gather(arrived, "tensor", axis=2, tiled=True)
    row_count = experts * capacity
    layout_ids = topology[0]
    blocked = expert_in.reshape(row_count, width // BLK, BLK)
    width_ids = jnp.arange(width // BLK, dtype=jnp.int32)
    partial_value = jnp.zeros((row_count, width // BLK, BLK), F32)
    for block in range(layout_ids.shape[0]):
        chosen = layout_ids[block]
        picked = jnp.take(blocked, chosen, axis=1)
        gate_proj = jnp.einsum("rkc,kcf->rf", picked, gate_blocks[0, block], preferred_element_type=F32)
        up_proj = jnp.einsum("rkc,kcf->rf", picked, up_blocks[0, block], preferred_element_type=F32)
        hidden = (jax.nn.silu(gate_proj) * up_proj).astype(BF16)
        pieces = jnp.einsum("rf,kfc->rkc", hidden, down_blocks[0, block], preferred_element_type=F32)
        placer = (chosen[:, None] == width_ids[None, :]).astype(F32)
        partial_value = partial_value + jnp.einsum(
            "rkc,kb->rbc", pieces, placer, precision=lax.Precision.HIGHEST
        )
    partial_low = lax.optimization_barrier(partial_value.reshape(experts, capacity, width).astype(BF16))
    shares = lax.all_to_all(
        partial_low.reshape(1, experts, capacity, width), "tensor", split_axis=3, concat_axis=0, tiled=True
    )
    summed = jnp.sum(shares.astype(F32), axis=0)
    returned_rows = lax.all_to_all(summed, ("dp", "expert"), split_axis=0, concat_axis=0, tiled=True)
    flat_rows = returned_rows.reshape(row_count, returned_rows.shape[2])
    return combine_rows(flat_rows, target, combine_weights).astype(BF16)


CORE, XBIT, YBIT = 1, 2, 4
FLIPS = (0, XBIT, YBIT, XBIT | YBIT)
XOR = {k: [(i, i ^ k) for i in range(4)] for k in (1, 2, 3)}
HALVES = 2


def flip(value, bit):
    return lax.ppermute(value, "dp", [(i, i ^ bit) for i in range(lax.axis_size("dp"))])


def along(value, pairs):
    return lax.ppermute(value, "expert", pairs)


def exchange(messages):
    across = flip(messages[3], FLIPS[3])
    return [messages[0], flip(messages[1], FLIPS[1]), flip(messages[2], FLIPS[2]), across]


def hold(values, after):
    return list(lax.optimization_barrier(tuple(values) + tuple(after))[: len(values)])


def both(arrived, others):
    held = hold([arrived[3], arrived[1], arrived[2], arrived[0]] + list(others), [])
    return [held[3], held[1], held[2], held[0]], held[4:]


def add(*values):
    return functools.reduce(lambda a, b: a + b, [v.astype(F32) for v in values]).astype(BF16)


def column(meta, lane):
    at = lax.broadcasted_iota(jnp.int32, meta.shape, 1)
    return jnp.sum(jnp.where(at == lane, meta, 0.0), axis=1, keepdims=True)


def slots_of(meta, half, ids, experts, cap, weighted):
    place = lax.broadcasted_iota(jnp.int32, (meta.shape[0], len(FLIPS) * HALVES * cap), 1)
    terms = [0.0] * (3 if weighted else 1)
    for n in range(len(FLIPS)):
        rank = column(meta, 3 * experts + ids[n]).astype(jnp.int32)
        here = place == jnp.where(rank >= 0, rank + (n * HALVES + half) * cap, -1)
        for t in range(len(terms)):
            terms[t] = jnp.where(here, column(meta, t * experts + ids[n]) if weighted else 1.0, terms[t])
    return terms


def select_kernel(width, experts, cap, ids, near, far, *outs):
    hot = jnp.concatenate(
        [slots_of(ref[:, width:].astype(F32), half, ids, experts, cap, False)[0] for half, ref in enumerate((near, far))],
        axis=0,
    ).astype(BF16)
    each = HALVES * cap
    step = 4 * BLK
    for at in range(0, width, step):
        cols = slice(at, at + step)
        block = jnp.concatenate([near[:, cols], far[:, cols]], axis=0)
        picked = lax.dot_general(hot, block, (((0,), (0,)), ((), ())), preferred_element_type=F32).astype(BF16)
        for n, out in enumerate(outs):
            out[:, cols] = picked[n * each : (n + 1) * each]


def select(ids, near, far, width, experts, cap):
    return pl.pallas_call(
        functools.partial(select_kernel, width, experts, cap),
        out_shape=[jax.ShapeDtypeStruct((HALVES * cap, width), BF16)] * len(FLIPS),
        in_specs=[pl.BlockSpec(memory_space=pltpu.SMEM)] + [pl.BlockSpec(memory_space=pltpu.VMEM)] * 2,
        out_specs=[pl.BlockSpec(memory_space=pltpu.VMEM)] * len(FLIPS),
        compiler_params=pltpu.CompilerParams(vmem_limit_bytes=VMEM_LIMIT),
        name="select_rows",
    )(ids, near, far)


def gather_kernel(width, experts, cap, ids, *refs):
    blocks, (mine, theirs) = refs[: len(FLIPS) * HALVES], refs[len(FLIPS) * HALVES :]
    each = HALVES * cap
    place = lax.broadcasted_iota(jnp.int32, (blocks[0].shape[0], HALVES * each), 1)
    for n in range(len(FLIPS)):
        pair = blocks[n * HALVES : (n + 1) * HALVES]
        parts = []
        for half, ref in enumerate(pair):
            meta = ref[:, width:].astype(F32)
            here = None
            for which in range(2):
                rank = column(meta, 3 * experts + ids[which]).astype(jnp.int32)
                found = place == jnp.where(rank >= 0, rank + which * each + half * cap, -1)
                here = found if here is None else here | found
            parts.append(jnp.where(here, 1.0, 0.0))
        hot = jnp.concatenate(parts, axis=0).astype(BF16)
        step = 4 * BLK
        for at in range(0, width, step):
            cols = slice(at, at + step)
            block = jnp.concatenate([ref[:, cols] for ref in pair], axis=0)
            picked = lax.dot_general(hot, block, (((0,), (0,)), ((), ())), preferred_element_type=F32).astype(BF16)
            mine[n * each : (n + 1) * each, cols] = picked[:each]
            theirs[n * each : (n + 1) * each, cols] = picked[each:]


def gather(ids, blocks, width, experts, cap):
    shape = jax.ShapeDtypeStruct((len(FLIPS) * HALVES * cap, width), BF16)
    return pl.pallas_call(
        functools.partial(gather_kernel, width, experts, cap),
        out_shape=[shape, shape],
        in_specs=[pl.BlockSpec(memory_space=pltpu.SMEM)] + [pl.BlockSpec(memory_space=pltpu.VMEM)] * len(blocks),
        out_specs=[pl.BlockSpec(memory_space=pltpu.VMEM)] * 2,
        compiler_params=pltpu.CompilerParams(vmem_limit_bytes=VMEM_LIMIT),
        name="gather_rows",
    )(ids, *blocks)


def combine_kernel(width, experts, cap, ids, near, far, *refs):
    rows, (mine, theirs) = refs[:4], refs[4:]
    halves = [slots_of(ref[:, ref.shape[1] - 4 * experts :].astype(F32), half, ids, experts, cap, True) for half, ref in enumerate((near, far))]
    terms = [jnp.concatenate(pair, axis=0).astype(BF16) for pair in zip(*halves)]
    tokens = near.shape[0]
    step = 4 * BLK
    for at in range(0, width, step):
        cols = slice(at, at + step)
        block = jnp.concatenate([ref[:, cols] for ref in rows], axis=0)
        total = functools.reduce(
            lambda a, b: a + b, [jnp.dot(term, block, preferred_element_type=F32) for term in terms]
        )
        mine[:, cols] = total[:tokens]
        theirs[:, cols] = total[tokens:].astype(BF16)


def combine(ids, near, far, rows, width, experts, cap):
    tokens = near.shape[0]
    return pl.pallas_call(
        functools.partial(combine_kernel, width, experts, cap),
        out_shape=[jax.ShapeDtypeStruct((tokens, width), F32), jax.ShapeDtypeStruct((tokens, width), BF16)],
        in_specs=[pl.BlockSpec(memory_space=pltpu.SMEM)] + [pl.BlockSpec(memory_space=pltpu.VMEM)] * 6,
        out_specs=[pl.BlockSpec(memory_space=pltpu.VMEM)] * 2,
        compiler_params=pltpu.CompilerParams(vmem_limit_bytes=VMEM_LIMIT),
        name="combine_rows",
    )(ids, near, far, *rows)


def expert_kernel(count, topo, *refs):
    inputs, (gate, up, down) = refs[:count], refs[count : count + 3]
    outputs, (x, total) = refs[count + 3 : -2], refs[-2:]
    h = pl.program_id(0)
    rows = inputs[0].shape[0]

    @pl.when(h == 0)
    def _():
        for n, ref in enumerate(inputs):
            x[n * rows : (n + 1) * rows, :] = ref[...]
        total[...] = jnp.zeros_like(total)

    _, each, kb, _, _ = gate.shape
    cols = [[pl.ds(pl.multiple_of(topo[h * each + n, i] * BLK, BLK), BLK) for i in range(kb)] for n in range(each)]
    hidden = []
    for n in range(each):
        picked = jnp.concatenate([x[:, c] for c in cols[n]], axis=1)
        weights = jnp.concatenate([gate[0, n].reshape(kb * BLK, BLK), up[0, n].reshape(kb * BLK, BLK)], axis=1)
        both = jnp.dot(picked, weights, preferred_element_type=F32)
        gate_proj, up_proj = both[:, :BLK], both[:, BLK:]
        hidden.append((gate_proj / (1.0 + jnp.exp(-gate_proj)) * up_proj).astype(BF16))
    for n in range(each):
        for i in range(0, kb, 2):
            pair = jnp.concatenate([down[0, n, i], down[0, n, i + 1]], axis=1)
            pieces = jnp.dot(hidden[n], pair, preferred_element_type=F32)
            total[:, cols[n][i]] += pieces[:, :BLK]
            total[:, cols[n][i + 1]] += pieces[:, BLK:]

    @pl.when(h == pl.num_programs(0) - 1)
    def _():
        each = outputs[0].shape[0]
        for n, out in enumerate(outputs):
            out[...] = total[n * each : (n + 1) * each, :].astype(BF16)


def expert(topo, inputs, weights):
    count, (rows, width) = len(inputs), inputs[0].shape
    _, blocks, kb, _, _ = weights[0].shape
    each = 3
    spec = pl.BlockSpec((1, each, kb, BLK, BLK), lambda h: (0, h, 0, 0, 0))
    whole = pl.BlockSpec((rows, width), lambda h: (0, 0))
    return pl.pallas_call(
        functools.partial(expert_kernel, count),
        grid=(blocks // each,),
        out_shape=[jax.ShapeDtypeStruct((count * rows // len(FLIPS), width), BF16)] * len(FLIPS),
        in_specs=[pl.BlockSpec(memory_space=pltpu.SMEM)] + [whole] * count + [spec] * 3,
        out_specs=[pl.BlockSpec((count * rows // len(FLIPS), width), lambda h: (0, 0))] * len(FLIPS),
        scratch_shapes=[pltpu.VMEM((count * rows, width), BF16), pltpu.VMEM((count * rows, width), F32)],
        compiler_params=pltpu.CompilerParams(vmem_limit_bytes=EXPERT_VMEM_LIMIT),
        name="expert_rows",
    )(topo, *inputs, *weights)


def with_meta(tokens, expert_ids, combine_weights, experts):
    rows = tokens.shape[0]
    named = expert_ids[:, :, None] == jnp.arange(experts, dtype=jnp.int32)[None, None, :]
    weight = jnp.sum(jnp.where(named, combine_weights[:, :, None], 0.0), axis=1)
    chosen = jnp.any(named, axis=1)
    earlier = jnp.tril(jnp.ones((rows, rows), BF16), -1)
    rank = jnp.dot(earlier, chosen.astype(BF16), preferred_element_type=F32)
    rank = jnp.where(chosen, rank, -1.0)
    high = lax.reduce_precision(weight, 8, 7)
    middle = lax.reduce_precision(weight - high, 8, 7)
    low = weight - high - middle
    meta = jnp.concatenate([v.astype(BF16) for v in (high, middle, low, rank)], axis=1)
    return jnp.concatenate([tokens, meta], axis=1), meta


def line_device(tokens, expert_ids, combine_weights, topology, gate_blocks, up_blocks, down_blocks):
    experts = lax.axis_size(("dp", "expert"))
    rows, width = tokens.shape
    cap = min(rows, 3 * rows * TOP // (2 * experts))
    dp, z = lax.axis_index("dp"), lax.axis_index("expert")
    ids = jnp.stack([(dp ^ bit) * lax.axis_size("expert") + z for bit in FLIPS]).astype(jnp.int32)
    topo = topology[0]
    weights = (gate_blocks, up_blocks, down_blocks)

    def chosen(near):
        far = flip(near, CORE)
        return (near, far), list(select(ids, near, far, width, experts, cap))

    def joined(pair, rows):
        mine, theirs = combine(ids, *pair, rows, width, experts, cap)
        return mine, flip(theirs, CORE)

    own, meta = with_meta(tokens, expert_ids, combine_weights, experts)
    near_ids = jnp.stack([ids[0], ids[0] ^ 1])

    own_far = flip(own, CORE)
    third = along(own, XOR[3])
    layer = exchange([own] * 4)
    layer, (third,) = both(layer, [third])

    pair3, out3 = chosen(third)
    late, *rest = hold([own] + layer + out3, [])
    layer, out3 = rest[:4], rest[4:]
    in3 = exchange(out3)
    second, first = along(late, XOR[2]), along(meta, XOR[1])
    halves = [own, own_far] + [half for near in layer[1:] for half in (near, flip(near, CORE))]
    in0, sent1 = gather(near_ids, halves, width, experts, cap)
    in3, (second, in0, sent1) = both(in3, [second, in0, sent1])

    pair2, out2 = chosen(second)
    sent1, *out2 = hold([sent1] + out2, [])
    in2 = exchange(out2)
    in1 = along(sent1, XOR[1])
    pair1 = first, flip(first, CORE)
    back3 = expert(topo, in3, weights)
    in2, back3 = both(in2, list(back3))

    got3 = exchange(back3)
    back2 = expert(topo, in2, weights)
    got3, back2 = both(got3, list(back2))

    got2 = exchange(back2)
    back0 = expert(topo, [in0], weights)
    in1, *back0 = hold([in1] + list(back0), [])
    back1 = expert(topo, [in1], weights)
    got2[3], *got3 = hold([got2[3]] + got3, [])
    mine3, theirs3 = combine(ids, *pair3, got3, width, experts, cap)
    got2, (mine3, theirs3, *back1) = both(got2, [mine3, theirs3] + list(back1))

    got1 = exchange(back1)
    far3 = along(add(mine3, flip(theirs3, CORE)), XOR[1])
    mine2, theirs2 = joined(pair2, got2)
    got1, (far3, mine2, theirs2, *back0) = both(got1, [far3, mine2, theirs2] + back0)

    got0 = exchange(back0)
    far2 = along(add(mine2, theirs2, far3), XOR[2])
    far1 = along(add(*joined(pair1, got1)), XOR[1])
    got0, (far1, far2) = both(got0, [far1, far2])
    mine0, theirs0 = joined((meta, flip(meta, CORE)), got0)
    return add(mine0, theirs0, far1, far2)


def solution(mesh):
    line = mesh.shape["dp"] == 8 and mesh.shape["expert"] == 4 and mesh.shape["tensor"] == 1
    return jax.shard_map(
        line_device if line else general_device,
        mesh=mesh,
        in_specs=(
            P(("dp", "expert"), "tensor"),
            P(("dp", "expert"), None),
            P(("dp", "expert"), None),
            P(("dp", "expert"), "tensor", None),
            P(("dp", "expert"), "tensor", None, None, None),
            P(("dp", "expert"), "tensor", None, None, None),
            P(("dp", "expert"), "tensor", None, None, None),
        ),
        out_specs=P(("dp", "expert"), "tensor"),
        check_vma=False,
    )
```

```python
import functools

import jax
import jax.numpy as jnp
from jax import lax
from jax.experimental import pallas as pl
from jax.experimental.pallas import tpu as pltpu
from jax.sharding import PartitionSpec as P

TOP = 8
BLK = 128
BF16 = jnp.bfloat16
F32 = jnp.float32
VMEM_LIMIT = 16 * 1024 * 1024
EXPERT_VMEM_LIMIT = 28 * 1024 * 1024


def slot_numbers(expert_ids, experts):
    flat_ids = expert_ids.reshape(-1)
    onehot = (flat_ids[:, None] == jnp.arange(experts, dtype=jnp.int32)[None, :]).astype(jnp.int32)
    before = jnp.cumsum(onehot, axis=0) - onehot
    return jnp.sum(before * onehot, axis=1).reshape(expert_ids.shape)


def combine_rows(flat_rows, target, combine_weights):
    total = jnp.zeros((target.shape[0], flat_rows.shape[1]), jnp.float32)
    for pick in range(target.shape[1]):
        chosen = jnp.take(flat_rows, target[:, pick], axis=0)
        total = total + combine_weights[:, pick][:, None] * chosen
    return total


def general_device(tokens, expert_ids, combine_weights, topology, gate_blocks, up_blocks, down_blocks):
    experts = lax.axis_size(("dp", "expert"))
    width = tokens.shape[1] * lax.axis_size("tensor")
    tok_rows = tokens.shape[0]
    capacity = min(tok_rows, 3 * tok_rows * TOP // (2 * experts))
    slot_index = slot_numbers(expert_ids, experts)
    target = expert_ids * capacity + slot_index
    places = jnp.arange(experts * capacity, dtype=jnp.int32)
    matches = target[None, :, :] == places[:, None, None]
    dispatch = jnp.any(matches, axis=2).astype(BF16)
    outgoing = jnp.dot(dispatch, tokens, preferred_element_type=F32).astype(BF16)
    outgoing = outgoing.reshape(experts, capacity, tokens.shape[1])
    arrived = lax.all_to_all(outgoing, ("dp", "expert"), split_axis=0, concat_axis=0, tiled=True)
    expert_in = lax.all_gather(arrived, "tensor", axis=2, tiled=True)
    row_count = experts * capacity
    layout_ids = topology[0]
    blocked = expert_in.reshape(row_count, width // BLK, BLK)
    width_ids = jnp.arange(width // BLK, dtype=jnp.int32)
    partial_value = jnp.zeros((row_count, width // BLK, BLK), F32)
    for block in range(layout_ids.shape[0]):
        chosen = layout_ids[block]
        picked = jnp.take(blocked, chosen, axis=1)
        gate_proj = jnp.einsum("rkc,kcf->rf", picked, gate_blocks[0, block], preferred_element_type=F32)
        up_proj = jnp.einsum("rkc,kcf->rf", picked, up_blocks[0, block], preferred_element_type=F32)
        hidden = (jax.nn.silu(gate_proj) * up_proj).astype(BF16)
        pieces = jnp.einsum("rf,kfc->rkc", hidden, down_blocks[0, block], preferred_element_type=F32)
        placer = (chosen[:, None] == width_ids[None, :]).astype(F32)
        partial_value = partial_value + jnp.einsum(
            "rkc,kb->rbc", pieces, placer, precision=lax.Precision.HIGHEST
        )
    partial_low = lax.optimization_barrier(partial_value.reshape(experts, capacity, width).astype(BF16))
    shares = lax.all_to_all(
        partial_low.reshape(1, experts, capacity, width), "tensor", split_axis=3, concat_axis=0, tiled=True
    )
    summed = jnp.sum(shares.astype(F32), axis=0)
    returned_rows = lax.all_to_all(summed, ("dp", "expert"), split_axis=0, concat_axis=0, tiled=True)
    flat_rows = returned_rows.reshape(row_count, returned_rows.shape[2])
    return combine_rows(flat_rows, target, combine_weights).astype(BF16)


CORE, XBIT, YBIT = 1, 2, 4
FLIPS = (0, XBIT, YBIT, XBIT | YBIT)
XOR = {k: [(i, i ^ k) for i in range(4)] for k in (1, 2, 3)}
HALVES = 2


def flip(value, bit):
    return lax.ppermute(value, "dp", [(i, i ^ bit) for i in range(lax.axis_size("dp"))])


def along(value, pairs):
    return lax.ppermute(value, "expert", pairs)


def exchange(messages):
    across = flip(messages[3], FLIPS[3])
    return [messages[0], flip(messages[1], FLIPS[1]), flip(messages[2], FLIPS[2]), across]


def hold(values, after):
    return list(lax.optimization_barrier(tuple(values) + tuple(after))[: len(values)])


def both(arrived, others):
    held = hold([arrived[3], arrived[1], arrived[2], arrived[0]] + list(others), [])
    return [held[3], held[1], held[2], held[0]], held[4:]


def add(*values):
    return functools.reduce(lambda a, b: a + b, [v.astype(F32) for v in values]).astype(BF16)


def column(meta, lane):
    at = lax.broadcasted_iota(jnp.int32, meta.shape, 1)
    return jnp.sum(jnp.where(at == lane, meta, 0.0), axis=1, keepdims=True)


def slots_of(meta, half, ids, experts, cap, weighted):
    place = lax.broadcasted_iota(jnp.int32, (meta.shape[0], len(FLIPS) * HALVES * cap), 1)
    terms = [0.0] * (3 if weighted else 1)
    for n in range(len(FLIPS)):
        rank = column(meta, 3 * experts + ids[n]).astype(jnp.int32)
        here = place == jnp.where(rank >= 0, rank + (n * HALVES + half) * cap, -1)
        for t in range(len(terms)):
            terms[t] = jnp.where(here, column(meta, t * experts + ids[n]) if weighted else 1.0, terms[t])
    return terms


def select_kernel(width, experts, cap, ids, near, far, *outs):
    hot = jnp.concatenate(
        [slots_of(ref[:, width:].astype(F32), half, ids, experts, cap, False)[0] for half, ref in enumerate((near, far))],
        axis=0,
    ).astype(BF16)
    each = HALVES * cap
    step = 4 * BLK
    for at in range(0, width, step):
        cols = slice(at, at + step)
        block = jnp.concatenate([near[:, cols], far[:, cols]], axis=0)
        picked = lax.dot_general(hot, block, (((0,), (0,)), ((), ())), preferred_element_type=F32).astype(BF16)
        for n, out in enumerate(outs):
            out[:, cols] = picked[n * each : (n + 1) * each]


def select(ids, near, far, width, experts, cap):
    return pl.pallas_call(
        functools.partial(select_kernel, width, experts, cap),
        out_shape=[jax.ShapeDtypeStruct((HALVES * cap, width), BF16)] * len(FLIPS),
        in_specs=[pl.BlockSpec(memory_space=pltpu.SMEM)] + [pl.BlockSpec(memory_space=pltpu.VMEM)] * 2,
        out_specs=[pl.BlockSpec(memory_space=pltpu.VMEM)] * len(FLIPS),
        compiler_params=pltpu.CompilerParams(vmem_limit_bytes=VMEM_LIMIT),
        name="select_rows",
    )(ids, near, far)


def gather_kernel(width, experts, cap, ids, *refs):
    blocks, (mine, theirs) = refs[: len(FLIPS) * HALVES], refs[len(FLIPS) * HALVES :]
    each = HALVES * cap
    place = lax.broadcasted_iota(jnp.int32, (blocks[0].shape[0], HALVES * each), 1)
    for n in range(len(FLIPS)):
        pair = blocks[n * HALVES : (n + 1) * HALVES]
        parts = []
        for half, ref in enumerate(pair):
            meta = ref[:, width:].astype(F32)
            here = None
            for which in range(2):
                rank = column(meta, 3 * experts + ids[which]).astype(jnp.int32)
                found = place == jnp.where(rank >= 0, rank + which * each + half * cap, -1)
                here = found if here is None else here | found
            parts.append(jnp.where(here, 1.0, 0.0))
        hot = jnp.concatenate(parts, axis=0).astype(BF16)
        step = 4 * BLK
        for at in range(0, width, step):
            cols = slice(at, at + step)
            block = jnp.concatenate([ref[:, cols] for ref in pair], axis=0)
            picked = lax.dot_general(hot, block, (((0,), (0,)), ((), ())), preferred_element_type=F32).astype(BF16)
            mine[n * each : (n + 1) * each, cols] = picked[:each]
            theirs[n * each : (n + 1) * each, cols] = picked[each:]


def gather(ids, blocks, width, experts, cap):
    shape = jax.ShapeDtypeStruct((len(FLIPS) * HALVES * cap, width), BF16)
    return pl.pallas_call(
        functools.partial(gather_kernel, width, experts, cap),
        out_shape=[shape, shape],
        in_specs=[pl.BlockSpec(memory_space=pltpu.SMEM)] + [pl.BlockSpec(memory_space=pltpu.VMEM)] * len(blocks),
        out_specs=[pl.BlockSpec(memory_space=pltpu.VMEM)] * 2,
        compiler_params=pltpu.CompilerParams(vmem_limit_bytes=VMEM_LIMIT),
        name="gather_rows",
    )(ids, *blocks)


def combine_kernel(width, experts, cap, ids, near, far, *refs):
    rows, (mine, theirs) = refs[:4], refs[4:]
    halves = [slots_of(ref[:, ref.shape[1] - 4 * experts :].astype(F32), half, ids, experts, cap, True) for half, ref in enumerate((near, far))]
    terms = [jnp.concatenate(pair, axis=0).astype(BF16) for pair in zip(*halves)]
    tokens = near.shape[0]
    step = 4 * BLK
    for at in range(0, width, step):
        cols = slice(at, at + step)
        block = jnp.concatenate([ref[:, cols] for ref in rows], axis=0)
        total = functools.reduce(
            lambda a, b: a + b, [jnp.dot(term, block, preferred_element_type=F32) for term in terms]
        )
        mine[:, cols] = total[:tokens]
        theirs[:, cols] = total[tokens:].astype(BF16)


def combine(ids, near, far, rows, width, experts, cap):
    tokens = near.shape[0]
    return pl.pallas_call(
        functools.partial(combine_kernel, width, experts, cap),
        out_shape=[jax.ShapeDtypeStruct((tokens, width), F32), jax.ShapeDtypeStruct((tokens, width), BF16)],
        in_specs=[pl.BlockSpec(memory_space=pltpu.SMEM)] + [pl.BlockSpec(memory_space=pltpu.VMEM)] * 6,
        out_specs=[pl.BlockSpec(memory_space=pltpu.VMEM)] * 2,
        compiler_params=pltpu.CompilerParams(vmem_limit_bytes=VMEM_LIMIT),
        name="combine_rows",
    )(ids, near, far, *rows)


def expert_kernel(count, topo, *refs):
    inputs, (gate, up, down) = refs[:count], refs[count : count + 3]
    outputs, (x, total) = refs[count + 3 : -2], refs[-2:]
    h = pl.program_id(0)
    rows = inputs[0].shape[0]

    @pl.when(h == 0)
    def _():
        for n, ref in enumerate(inputs):
            x[n * rows : (n + 1) * rows, :] = ref[...]
        total[...] = jnp.zeros_like(total)

    _, each, kb, _, _ = gate.shape
    cols = [[pl.ds(pl.multiple_of(topo[h * each + n, i] * BLK, BLK), BLK) for i in range(kb)] for n in range(each)]
    hidden = []
    for n in range(each):
        picked = jnp.concatenate([x[:, c] for c in cols[n]], axis=1)
        weights = jnp.concatenate([gate[0, n].reshape(kb * BLK, BLK), up[0, n].reshape(kb * BLK, BLK)], axis=1)
        both = jnp.dot(picked, weights, preferred_element_type=F32)
        gate_proj, up_proj = both[:, :BLK], both[:, BLK:]
        hidden.append((gate_proj / (1.0 + jnp.exp(-gate_proj)) * up_proj).astype(BF16))
    for n in range(each):
        for i in range(0, kb, 2):
            pair = jnp.concatenate([down[0, n, i], down[0, n, i + 1]], axis=1)
            pieces = jnp.dot(hidden[n], pair, preferred_element_type=F32)
            total[:, cols[n][i]] += pieces[:, :BLK]
            total[:, cols[n][i + 1]] += pieces[:, BLK:]

    @pl.when(h == pl.num_programs(0) - 1)
    def _():
        each = outputs[0].shape[0]
        for n, out in enumerate(outputs):
            out[...] = total[n * each : (n + 1) * each, :].astype(BF16)


def expert(topo, inputs, weights):
    count, (rows, width) = len(inputs), inputs[0].shape
    _, blocks, kb, _, _ = weights[0].shape
    each = 3
    spec = pl.BlockSpec((1, each, kb, BLK, BLK), lambda h: (0, h, 0, 0, 0))
    whole = pl.BlockSpec((rows, width), lambda h: (0, 0))
    return pl.pallas_call(
        functools.partial(expert_kernel, count),
        grid=(blocks // each,),
        out_shape=[jax.ShapeDtypeStruct((count * rows // len(FLIPS), width), BF16)] * len(FLIPS),
        in_specs=[pl.BlockSpec(memory_space=pltpu.SMEM)] + [whole] * count + [spec] * 3,
        out_specs=[pl.BlockSpec((count * rows // len(FLIPS), width), lambda h: (0, 0))] * len(FLIPS),
        scratch_shapes=[pltpu.VMEM((count * rows, width), BF16), pltpu.VMEM((count * rows, width), F32)],
        compiler_params=pltpu.CompilerParams(vmem_limit_bytes=EXPERT_VMEM_LIMIT),
        name="expert_rows",
    )(topo, *inputs, *weights)


def with_meta(tokens, expert_ids, combine_weights, experts):
    rows = tokens.shape[0]
    named = expert_ids[:, :, None] == jnp.arange(experts, dtype=jnp.int32)[None, None, :]
    weight = jnp.sum(jnp.where(named, combine_weights[:, :, None], 0.0), axis=1)
    chosen = jnp.any(named, axis=1)
    earlier = jnp.tril(jnp.ones((rows, rows), BF16), -1)
    rank = jnp.dot(earlier, chosen.astype(BF16), preferred_element_type=F32)
    rank = jnp.where(chosen, rank, -1.0)
    high = lax.reduce_precision(weight, 8, 7)
    middle = lax.reduce_precision(weight - high, 8, 7)
    low = weight - high - middle
    meta = jnp.concatenate([v.astype(BF16) for v in (high, middle, low, rank)], axis=1)
    return jnp.concatenate([tokens, meta], axis=1), meta


def line_device(tokens, expert_ids, combine_weights, topology, gate_blocks, up_blocks, down_blocks):
    experts = lax.axis_size(("dp", "expert"))
    rows, width = tokens.shape
    cap = min(rows, 3 * rows * TOP // (2 * experts))
    dp, z = lax.axis_index("dp"), lax.axis_index("expert")
    ids = jnp.stack([(dp ^ bit) * lax.axis_size("expert") + z for bit in FLIPS]).astype(jnp.int32)
    topo = topology[0]
    weights = (gate_blocks, up_blocks, down_blocks)

    def chosen(near):
        far = flip(near, CORE)
        return (near, far), list(select(ids, near, far, width, experts, cap))

    def joined(pair, rows):
        mine, theirs = combine(ids, *pair, rows, width, experts, cap)
        return mine, flip(theirs, CORE)

    own, meta = with_meta(tokens, expert_ids, combine_weights, experts)
    near_ids = jnp.stack([ids[0], ids[0] ^ 1])

    own_far = flip(own, CORE)
    third = along(own, XOR[3])
    layer = exchange([own] * 4)
    layer, (third, late) = both(layer, [third, own])

    pair3, out3 = chosen(third)
    in3 = exchange(out3)
    second, first = along(late, XOR[2]), along(meta, XOR[1])
    halves = [own, own_far] + [half for near in layer[1:] for half in (near, flip(near, CORE))]
    in0, sent1 = gather(near_ids, halves, width, experts, cap)
    in3, (second, in0, sent1) = both(in3, [second, in0, sent1])

    pair2, out2 = chosen(second)
    sent1, *out2 = hold([sent1] + out2, [])
    in2 = exchange(out2)
    in1 = along(sent1, XOR[1])
    pair1 = first, flip(first, CORE)
    back3 = expert(topo, in3, weights)
    in2, back3 = both(in2, list(back3))

    got3 = exchange(back3)
    back2 = expert(topo, in2, weights)
    got3, back2 = both(got3, list(back2))

    got2 = exchange(back2)
    back0 = expert(topo, [in0], weights)
    in1, *back0 = hold([in1] + list(back0), [])
    back1 = expert(topo, [in1], weights)
    got2[3], *got3 = hold([got2[3]] + got3, [])
    mine3, theirs3 = combine(ids, *pair3, got3, width, experts, cap)
    got2, (mine3, theirs3, *back1) = both(got2, [mine3, theirs3] + list(back1))

    got1 = exchange(back1)
    far3 = along(add(mine3, flip(theirs3, CORE)), XOR[1])
    mine2, theirs2 = joined(pair2, got2)
    got1, (far3, mine2, theirs2, *back0) = both(got1, [far3, mine2, theirs2] + back0)

    got0 = exchange(back0)
    far2 = along(add(mine2, theirs2, far3), XOR[2])
    far1 = along(add(*joined(pair1, got1)), XOR[1])
    got0, (far1, far2) = both(got0, [far1, far2])
    mine0, theirs0 = joined((meta, flip(meta, CORE)), got0)
    return add(mine0, theirs0, far1, far2)


def solution(mesh):
    line = mesh.shape["dp"] == 8 and mesh.shape["expert"] == 4 and mesh.shape["tensor"] == 1
    return jax.shard_map(
        line_device if line else general_device,
        mesh=mesh,
        in_specs=(
            P(("dp", "expert"), "tensor"),
            P(("dp", "expert"), None),
            P(("dp", "expert"), None),
            P(("dp", "expert"), "tensor", None),
            P(("dp", "expert"), "tensor", None, None, None),
            P(("dp", "expert"), "tensor", None, None, None),
            P(("dp", "expert"), "tensor", None, None, None),
        ),
        out_specs=P(("dp", "expert"), "tensor"),
        check_vma=False,
    )
```

```python
import functools

import jax
import jax.numpy as jnp
from jax import lax
from jax.experimental import pallas as pl
from jax.experimental.pallas import tpu as pltpu
from jax.sharding import PartitionSpec as P

TOP = 8
BLK = 128
BF16 = jnp.bfloat16
F32 = jnp.float32
VMEM_LIMIT = 16 * 1024 * 1024
EXPERT_VMEM_LIMIT = 28 * 1024 * 1024


def slot_numbers(expert_ids, experts):
    flat_ids = expert_ids.reshape(-1)
    onehot = (flat_ids[:, None] == jnp.arange(experts, dtype=jnp.int32)[None, :]).astype(jnp.int32)
    before = jnp.cumsum(onehot, axis=0) - onehot
    return jnp.sum(before * onehot, axis=1).reshape(expert_ids.shape)


def combine_rows(flat_rows, target, combine_weights):
    total = jnp.zeros((target.shape[0], flat_rows.shape[1]), jnp.float32)
    for pick in range(target.shape[1]):
        chosen = jnp.take(flat_rows, target[:, pick], axis=0)
        total = total + combine_weights[:, pick][:, None] * chosen
    return total


def general_device(tokens, expert_ids, combine_weights, topology, gate_blocks, up_blocks, down_blocks):
    experts = lax.axis_size(("dp", "expert"))
    width = tokens.shape[1] * lax.axis_size("tensor")
    tok_rows = tokens.shape[0]
    capacity = min(tok_rows, 3 * tok_rows * TOP // (2 * experts))
    slot_index = slot_numbers(expert_ids, experts)
    target = expert_ids * capacity + slot_index
    places = jnp.arange(experts * capacity, dtype=jnp.int32)
    matches = target[None, :, :] == places[:, None, None]
    dispatch = jnp.any(matches, axis=2).astype(BF16)
    outgoing = jnp.dot(dispatch, tokens, preferred_element_type=F32).astype(BF16)
    outgoing = outgoing.reshape(experts, capacity, tokens.shape[1])
    arrived = lax.all_to_all(outgoing, ("dp", "expert"), split_axis=0, concat_axis=0, tiled=True)
    expert_in = lax.all_gather(arrived, "tensor", axis=2, tiled=True)
    row_count = experts * capacity
    layout_ids = topology[0]
    blocked = expert_in.reshape(row_count, width // BLK, BLK)
    width_ids = jnp.arange(width // BLK, dtype=jnp.int32)
    partial_value = jnp.zeros((row_count, width // BLK, BLK), F32)
    for block in range(layout_ids.shape[0]):
        chosen = layout_ids[block]
        picked = jnp.take(blocked, chosen, axis=1)
        gate_proj = jnp.einsum("rkc,kcf->rf", picked, gate_blocks[0, block], preferred_element_type=F32)
        up_proj = jnp.einsum("rkc,kcf->rf", picked, up_blocks[0, block], preferred_element_type=F32)
        hidden = (jax.nn.silu(gate_proj) * up_proj).astype(BF16)
        pieces = jnp.einsum("rf,kfc->rkc", hidden, down_blocks[0, block], preferred_element_type=F32)
        placer = (chosen[:, None] == width_ids[None, :]).astype(F32)
        partial_value = partial_value + jnp.einsum(
            "rkc,kb->rbc", pieces, placer, precision=lax.Precision.HIGHEST
        )
    partial_low = lax.optimization_barrier(partial_value.reshape(experts, capacity, width).astype(BF16))
    shares = lax.all_to_all(
        partial_low.reshape(1, experts, capacity, width), "tensor", split_axis=3, concat_axis=0, tiled=True
    )
    summed = jnp.sum(shares.astype(F32), axis=0)
    returned_rows = lax.all_to_all(summed, ("dp", "expert"), split_axis=0, concat_axis=0, tiled=True)
    flat_rows = returned_rows.reshape(row_count, returned_rows.shape[2])
    return combine_rows(flat_rows, target, combine_weights).astype(BF16)


CORE, XBIT, YBIT = 1, 2, 4
FLIPS = (0, XBIT, YBIT, XBIT | YBIT)
XOR = {k: [(i, i ^ k) for i in range(4)] for k in (1, 2, 3)}
HALVES = 2


def flip(value, bit):
    return lax.ppermute(value, "dp", [(i, i ^ bit) for i in range(lax.axis_size("dp"))])


def along(value, pairs):
    return lax.ppermute(value, "expert", pairs)


def exchange(messages):
    across = flip(messages[3], FLIPS[3])
    return [messages[0], flip(messages[1], FLIPS[1]), flip(messages[2], FLIPS[2]), across]


def hold(values, after):
    return list(lax.optimization_barrier(tuple(values) + tuple(after))[: len(values)])


def both(arrived, others):
    held = hold([arrived[3], arrived[1], arrived[2], arrived[0]] + list(others), [])
    return [held[3], held[1], held[2], held[0]], held[4:]


def add(*values):
    return functools.reduce(lambda a, b: a + b, [v.astype(F32) for v in values]).astype(BF16)


def column(meta, lane):
    at = lax.broadcasted_iota(jnp.int32, meta.shape, 1)
    return jnp.sum(jnp.where(at == lane, meta, 0.0), axis=1, keepdims=True)


def slots_of(meta, half, ids, experts, cap, weighted):
    place = lax.broadcasted_iota(jnp.int32, (meta.shape[0], len(FLIPS) * HALVES * cap), 1)
    terms = [0.0] * (3 if weighted else 1)
    for n in range(len(FLIPS)):
        rank = column(meta, 3 * experts + ids[n]).astype(jnp.int32)
        here = place == jnp.where(rank >= 0, rank + (n * HALVES + half) * cap, -1)
        for t in range(len(terms)):
            terms[t] = jnp.where(here, column(meta, t * experts + ids[n]) if weighted else 1.0, terms[t])
    return terms


def select_kernel(width, experts, cap, ids, near, far, *outs):
    hot = jnp.concatenate(
        [slots_of(ref[:, width:].astype(F32), half, ids, experts, cap, False)[0] for half, ref in enumerate((near, far))],
        axis=0,
    ).astype(BF16)
    each = HALVES * cap
    step = 4 * BLK
    for at in range(0, width, step):
        cols = slice(at, at + step)
        block = jnp.concatenate([near[:, cols], far[:, cols]], axis=0)
        picked = lax.dot_general(hot, block, (((0,), (0,)), ((), ())), preferred_element_type=F32).astype(BF16)
        for n, out in enumerate(outs):
            out[:, cols] = picked[n * each : (n + 1) * each]


def select(ids, near, far, width, experts, cap):
    return pl.pallas_call(
        functools.partial(select_kernel, width, experts, cap),
        out_shape=[jax.ShapeDtypeStruct((HALVES * cap, width), BF16)] * len(FLIPS),
        in_specs=[pl.BlockSpec(memory_space=pltpu.SMEM)] + [pl.BlockSpec(memory_space=pltpu.VMEM)] * 2,
        out_specs=[pl.BlockSpec(memory_space=pltpu.VMEM)] * len(FLIPS),
        compiler_params=pltpu.CompilerParams(vmem_limit_bytes=VMEM_LIMIT),
        name="select_rows",
    )(ids, near, far)


def gather_kernel(width, experts, cap, ids, *refs):
    blocks, (mine, theirs) = refs[: len(FLIPS) * HALVES], refs[len(FLIPS) * HALVES :]
    each = HALVES * cap
    place = lax.broadcasted_iota(jnp.int32, (blocks[0].shape[0], HALVES * each), 1)
    for n in range(len(FLIPS)):
        pair = blocks[n * HALVES : (n + 1) * HALVES]
        parts = []
        for half, ref in enumerate(pair):
            meta = ref[:, width:].astype(F32)
            here = None
            for which in range(2):
                rank = column(meta, 3 * experts + ids[which]).astype(jnp.int32)
                found = place == jnp.where(rank >= 0, rank + which * each + half * cap, -1)
                here = found if here is None else here | found
            parts.append(jnp.where(here, 1.0, 0.0))
        hot = jnp.concatenate(parts, axis=0).astype(BF16)
        step = 4 * BLK
        for at in range(0, width, step):
            cols = slice(at, at + step)
            block = jnp.concatenate([ref[:, cols] for ref in pair], axis=0)
            picked = lax.dot_general(hot, block, (((0,), (0,)), ((), ())), preferred_element_type=F32).astype(BF16)
            mine[n * each : (n + 1) * each, cols] = picked[:each]
            theirs[n * each : (n + 1) * each, cols] = picked[each:]


def gather(ids, blocks, width, experts, cap):
    shape = jax.ShapeDtypeStruct((len(FLIPS) * HALVES * cap, width), BF16)
    return pl.pallas_call(
        functools.partial(gather_kernel, width, experts, cap),
        out_shape=[shape, shape],
        in_specs=[pl.BlockSpec(memory_space=pltpu.SMEM)] + [pl.BlockSpec(memory_space=pltpu.VMEM)] * len(blocks),
        out_specs=[pl.BlockSpec(memory_space=pltpu.VMEM)] * 2,
        compiler_params=pltpu.CompilerParams(vmem_limit_bytes=VMEM_LIMIT),
        name="gather_rows",
    )(ids, *blocks)


def combine_kernel(width, experts, cap, ids, near, far, *refs):
    rows, (mine, theirs) = refs[:4], refs[4:]
    halves = [slots_of(ref[:, ref.shape[1] - 4 * experts :].astype(F32), half, ids, experts, cap, True) for half, ref in enumerate((near, far))]
    terms = [jnp.concatenate(pair, axis=0).astype(BF16) for pair in zip(*halves)]
    tokens = near.shape[0]
    step = 4 * BLK
    for at in range(0, width, step):
        cols = slice(at, at + step)
        block = jnp.concatenate([ref[:, cols] for ref in rows], axis=0)
        total = functools.reduce(
            lambda a, b: a + b, [jnp.dot(term, block, preferred_element_type=F32) for term in terms]
        )
        mine[:, cols] = total[:tokens]
        theirs[:, cols] = total[tokens:].astype(BF16)


def combine(ids, near, far, rows, width, experts, cap):
    tokens = near.shape[0]
    return pl.pallas_call(
        functools.partial(combine_kernel, width, experts, cap),
        out_shape=[jax.ShapeDtypeStruct((tokens, width), F32), jax.ShapeDtypeStruct((tokens, width), BF16)],
        in_specs=[pl.BlockSpec(memory_space=pltpu.SMEM)] + [pl.BlockSpec(memory_space=pltpu.VMEM)] * 6,
        out_specs=[pl.BlockSpec(memory_space=pltpu.VMEM)] * 2,
        compiler_params=pltpu.CompilerParams(vmem_limit_bytes=VMEM_LIMIT),
        name="combine_rows",
    )(ids, near, far, *rows)


def expert_kernel(count, topo, *refs):
    inputs, (gate, up, down) = refs[:count], refs[count : count + 3]
    outputs, (x, total) = refs[count + 3 : -2], refs[-2:]
    h = pl.program_id(0)
    rows = inputs[0].shape[0]

    @pl.when(h == 0)
    def _():
        for n, ref in enumerate(inputs):
            x[n * rows : (n + 1) * rows, :] = ref[...]
        total[...] = jnp.zeros_like(total)

    _, each, kb, _, _ = gate.shape
    cols = [[pl.ds(pl.multiple_of(topo[h * each + n, i] * BLK, BLK), BLK) for i in range(kb)] for n in range(each)]
    hidden = []
    for n in range(each):
        picked = jnp.concatenate([x[:, c] for c in cols[n]], axis=1)
        weights = jnp.concatenate([gate[0, n].reshape(kb * BLK, BLK), up[0, n].reshape(kb * BLK, BLK)], axis=1)
        both = jnp.dot(picked, weights, preferred_element_type=F32)
        gate_proj, up_proj = both[:, :BLK], both[:, BLK:]
        hidden.append((gate_proj / (1.0 + jnp.exp(-gate_proj)) * up_proj).astype(BF16))
    for n in range(each):
        for i in range(0, kb, 2):
            pair = jnp.concatenate([down[0, n, i], down[0, n, i + 1]], axis=1)
            pieces = jnp.dot(hidden[n], pair, preferred_element_type=F32)
            total[:, cols[n][i]] += pieces[:, :BLK]
            total[:, cols[n][i + 1]] += pieces[:, BLK:]

    @pl.when(h == pl.num_programs(0) - 1)
    def _():
        each = outputs[0].shape[0]
        for n, out in enumerate(outputs):
            out[...] = total[n * each : (n + 1) * each, :].astype(BF16)


def expert(topo, inputs, weights):
    count, (rows, width) = len(inputs), inputs[0].shape
    _, blocks, kb, _, _ = weights[0].shape
    each = 3
    spec = pl.BlockSpec((1, each, kb, BLK, BLK), lambda h: (0, h, 0, 0, 0))
    whole = pl.BlockSpec((rows, width), lambda h: (0, 0))
    return pl.pallas_call(
        functools.partial(expert_kernel, count),
        grid=(blocks // each,),
        out_shape=[jax.ShapeDtypeStruct((count * rows // len(FLIPS), width), BF16)] * len(FLIPS),
        in_specs=[pl.BlockSpec(memory_space=pltpu.SMEM)] + [whole] * count + [spec] * 3,
        out_specs=[pl.BlockSpec((count * rows // len(FLIPS), width), lambda h: (0, 0))] * len(FLIPS),
        scratch_shapes=[pltpu.VMEM((count * rows, width), BF16), pltpu.VMEM((count * rows, width), F32)],
        compiler_params=pltpu.CompilerParams(vmem_limit_bytes=EXPERT_VMEM_LIMIT),
        name="expert_rows",
    )(topo, *inputs, *weights)


def with_meta(tokens, expert_ids, combine_weights, experts):
    rows = tokens.shape[0]
    named = expert_ids[:, :, None] == jnp.arange(experts, dtype=jnp.int32)[None, None, :]
    weight = jnp.sum(jnp.where(named, combine_weights[:, :, None], 0.0), axis=1)
    chosen = jnp.any(named, axis=1)
    earlier = jnp.tril(jnp.ones((rows, rows), BF16), -1)
    rank = jnp.dot(earlier, chosen.astype(BF16), preferred_element_type=F32)
    rank = jnp.where(chosen, rank, -1.0)
    high = lax.reduce_precision(weight, 8, 7)
    middle = lax.reduce_precision(weight - high, 8, 7)
    low = weight - high - middle
    meta = jnp.concatenate([v.astype(BF16) for v in (high, middle, low, rank)], axis=1)
    return jnp.concatenate([tokens, meta], axis=1), meta


def line_device(tokens, expert_ids, combine_weights, topology, gate_blocks, up_blocks, down_blocks):
    experts = lax.axis_size(("dp", "expert"))
    rows, width = tokens.shape
    cap = min(rows, 3 * rows * TOP // (2 * experts))
    dp, z = lax.axis_index("dp"), lax.axis_index("expert")
    ids = jnp.stack([(dp ^ bit) * lax.axis_size("expert") + z for bit in FLIPS]).astype(jnp.int32)
    topo = topology[0]
    weights = (gate_blocks, up_blocks, down_blocks)

    def chosen(near):
        far = flip(near, CORE)
        return (near, far), list(select(ids, near, far, width, experts, cap))

    def joined(pair, rows):
        mine, theirs = combine(ids, *pair, rows, width, experts, cap)
        return mine, flip(theirs, CORE)

    own, meta = with_meta(tokens, expert_ids, combine_weights, experts)
    near_ids = jnp.stack([ids[0], ids[0] ^ 1])

    own_far = flip(own, CORE)
    third = along(own, XOR[3])
    layer = exchange([own] * 4)
    layer, (third, late) = both(layer, [third, own])

    pair3, out3 = chosen(third)
    in3 = exchange(out3)
    second, first = along(late, XOR[2]), along(meta, XOR[1])
    halves = [own, own_far] + [half for near in layer[1:] for half in (near, flip(near, CORE))]
    in0, sent1 = gather(near_ids, halves, width, experts, cap)
    in3, (second, in0, sent1) = both(in3, [second, in0, sent1])

    pair2, out2 = chosen(second)
    sent1, *out2 = hold([sent1] + out2, [])
    in2 = exchange(out2)
    in1 = along(sent1, XOR[1])
    pair1 = first, flip(first, CORE)
    back3 = expert(topo, in3, weights)
    in2, back3 = both(in2, list(back3))

    got3 = exchange(back3)
    back2 = expert(topo, in2, weights)
    got3, held = both(got3, list(pair1) + list(back2))
    pair1, back2 = held[:2], held[2:]

    got2 = exchange(back2)
    back0 = expert(topo, [in0], weights)
    in1, *back0 = hold([in1] + list(back0), [])
    back1 = expert(topo, [in1], weights)
    got2[3], *got3 = hold([got2[3]] + got3, [])
    mine3, theirs3 = combine(ids, *pair3, got3, width, experts, cap)
    got2, (mine3, theirs3, *back1) = both(got2, [mine3, theirs3] + list(back1))

    got1 = exchange(back1)
    far3 = along(add(mine3, flip(theirs3, CORE)), XOR[1])
    mine2, theirs2 = combine(ids, *pair2, got2, width, experts, cap)
    got1, (far3, mine2, theirs2, *back0) = both(got1, [far3, mine2, theirs2] + back0)
    theirs2 = flip(theirs2, CORE)

    got0 = exchange(back0)
    far2 = along(add(mine2, theirs2, far3), XOR[2])
    far1 = along(add(*joined(pair1, got1)), XOR[1])
    got0, (far1, far2) = both(got0, [far1, far2])
    mine0, theirs0 = joined((meta, flip(meta, CORE)), got0)
    return add(mine0, theirs0, far1, far2)


def solution(mesh):
    line = mesh.shape["dp"] == 8 and mesh.shape["expert"] == 4 and mesh.shape["tensor"] == 1
    return jax.shard_map(
        line_device if line else general_device,
        mesh=mesh,
        in_specs=(
            P(("dp", "expert"), "tensor"),
            P(("dp", "expert"), None),
            P(("dp", "expert"), None),
            P(("dp", "expert"), "tensor", None),
            P(("dp", "expert"), "tensor", None, None, None),
            P(("dp", "expert"), "tensor", None, None, None),
            P(("dp", "expert"), "tensor", None, None, None),
        ),
        out_specs=P(("dp", "expert"), "tensor"),
        check_vma=False,
    )
```
